768 devices in a mesh: dp: 96 (over x, z, core), section: 8 (over y).
Axes of the slice: x: 4, y: 8, z: 12, core: 2. Of those that a mesh axis runs over, the one named last changes fastest.
Arguments:
- grads: bfloat16 [96, 2, 8, 6144, 128], P('dp', None, 'section'), may hold values from -3.5 to 3.5
- params: float32 [8, 6144, 128], P('section', 'dp'), may hold values from -4 to 4
- first_moment: float32 [8, 6144, 128], P('section', 'dp'), may hold values from -1.5 to 1.5
- second_moment: float32 [8, 6144, 128], P('section', 'dp'), may hold values from 0.01 to 0.2
- owners: int32 [96, 8, 8], P('dp', 'section'), may hold values from 0 to 7, as said below
Outputs:
- ckpt_param: float32 [96, 2048, 128], P('dp', 'section')
- ckpt_first: float32 [96, 2048, 128], P('dp', 'section')
- ckpt_second: float32 [96, 2048, 128], P('dp', 'section')
The draws below stay inside these ranges and needn't reach their ends.
Inputs may be any that keep to these rules, and one draw needn't show every extreme that they name: `owners`: each device names a writer for each of its 8 pieces and names no writer more than 4 times; in each group of devices sharing a dp index, one writer is named exactly 4 times by every device of the group.
All inputs are finite; a program needn't handle non-finite values.
Results may differ from the reference program's by a relative error of at most 0.0003.
Values sent between devices are 32-bit elements; how exact they have to be, the bound alone decides.
No kernel may reach another device: no remote copies, remote signals or barrier semaphores. Data moves between devices by JAX's collectives and lax.ppermute only.
A program may use at most 32 MiB of HBM per device.

```python
import math
import jax
import jax.numpy as jnp
from jax import lax

LANE = 128
PIECES = 8
MICRO = 2
CAP = 4
BUCKET_ROWS = 6144
N_DP = 96
N_SECTION = 8


def draw_owners(key, part):
    key = jax.random.fold_in(key, 7)
    key_hot, key_order, key_rest = jax.random.split(key, 3)
    hot_writer = jax.random.randint(key_hot, (N_DP, 1, 1), 0, N_SECTION)
    scores = jax.random.randint(key_order, (N_DP, N_SECTION, PIECES), 0, 1 << 20)
    scores = scores * PIECES + jnp.arange(PIECES, dtype=jnp.int32)
    ranking = jnp.argsort(jnp.argsort(scores, axis=-1, stable=True), axis=-1, stable=True)
    elsewhere = (hot_writer + 1 + jax.random.randint(key_rest, (N_DP, N_SECTION, PIECES), 0, N_SECTION - 1)) % N_SECTION
    return jnp.where(ranking < CAP, hot_writer, elsewhere).astype(jnp.int32)


def with_spikes(result, rng, source, target, blocks, factor):
    def block_of(dim):
        return (jnp.arange(result.shape[dim]) // (result.shape[dim] // blocks)).reshape((-1,) + (1,) * (result.ndim - 1 - dim))

    one_side = jax.random.permutation(rng, blocks)[block_of(target)]
    second = (block_of(target) + blocks // 2) % blocks
    return jnp.where((block_of(source) == one_side) | (block_of(source) == second), factor * result, result)


def level_of(own_key, shape, cuts, smallest, top_value):
    factor_of, own = 1.0, jax.random.fold_in(own_key, 6)
    for dim, blocks in cuts:
        draws = jnp.exp(jax.random.uniform(jax.random.fold_in(own, dim), (blocks,), jnp.float32, smallest / len(cuts), top_value / len(cuts)))
        factor_of = factor_of * jnp.repeat(draws, shape[dim] // blocks).reshape([-1 if axis == dim else 1 for axis in range(len(shape))])
    return factor_of


def centred(stream_key, dims, deviation, limit, cuts=(), kind=jnp.bfloat16):
    gain = level_of(stream_key, dims, cuts, -0.22, 0.18) if cuts else 1.0
    array = jax.random.normal(stream_key, dims, jnp.float32) * deviation * gain
    return jnp.minimum(jnp.maximum(array, -limit), limit).astype(kind)


def noise_with(key, extent, spread, most, cuts, heavy, held_as=jnp.bfloat16):
    drawn = spread * jax.random.normal(key, extent, jnp.float32)
    if cuts:
        drawn = drawn * level_of(key, extent, cuts, -0.22, 0.18)
    return jnp.clip(with_spikes(drawn, jax.random.fold_in(key, 3), *heavy), -most, most).astype(held_as)


def setup_inputs(seed: int = 0) -> dict:
    arg_keys = jax.random.split(jax.random.key(seed), 6)
    grads = noise_with(arg_keys[0], (N_DP, MICRO, N_SECTION, BUCKET_ROWS, LANE), 0.07, 3.5, ((0, 96), (2, 8)), (0, 3, 96, 4.75))
    params = centred(arg_keys[1], (N_SECTION, BUCKET_ROWS, LANE), 0.3, 4.0, ((0, 8), (1, 96)), jnp.float32)
    first_moment = centred(arg_keys[2], (N_SECTION, BUCKET_ROWS, LANE), 0.1, 1.5, ((0, 8), (1, 96)), jnp.float32)
    second_moment = jnp.clip(jnp.exp(math.log(0.2) - 2.9957323 * jax.random.uniform(arg_keys[3], (N_SECTION, BUCKET_ROWS, LANE), jnp.float32) ** level_of(arg_keys[3], (N_SECTION, BUCKET_ROWS, LANE), ((0, 8), (1, 96)), -0.2, 0.2)), 0.01, 0.2)
    owners = draw_owners(jax.random.fold_in(arg_keys[5], 71), 0)
    return {"grads": grads, "params": params, "first_moment": first_moment, "second_moment": second_moment, "owners": owners}


beta_one = 0.9
beta_two = 0.95
learn_rate = 0.03
decay_rate = 0.1
epsilon = 1e-08

def accumulate(total, partial_value):
    return (total + lax.optimization_barrier(jnp.sum(partial_value.astype(jnp.float32), axis=0)), None)

def reference(grads, params, first_moment, second_moment, owners):
    dp_count, micro_count, section_count, bucket, lane_count = grads.shape
    start_total = jnp.zeros((section_count, bucket, lane_count), jnp.float32)
    gradient, unused = lax.scan(accumulate, start_total, grads)
    momentum = beta_one * first_moment + (1.0 - beta_one) * gradient
    variance = beta_two * second_moment + (1.0 - beta_two) * gradient * gradient
    updated = params - learn_rate * (momentum / (jnp.sqrt(variance) + epsilon) + decay_rate * params)
    pieces = owners.shape[2]
    piece_rows = bucket // (dp_count * pieces)
    capacity = pieces // 2
    slot_count = section_count * capacity
    states = jnp.stack([updated, momentum, variance])
    states = states.reshape(3, section_count, dp_count, pieces, piece_rows, lane_count)
    states = jnp.transpose(states, (0, 2, 1, 3, 4, 5))
    writers = jnp.arange(section_count, dtype=jnp.int32)
    writer_hits = (owners[..., None] == writers).astype(jnp.int32)
    rank_within = jnp.cumsum(writer_hits, axis=2) - writer_hits
    totals = lax.optimization_barrier(jnp.sum(writer_hits, axis=2))
    starts = jnp.cumsum(totals, axis=1) - totals
    position = lax.optimization_barrier(jnp.sum(writer_hits * (rank_within + starts[:, :, None, :]), axis=3)).astype(jnp.int32)
    group_index = jnp.broadcast_to(jnp.arange(dp_count, dtype=jnp.int32)[:, None, None], owners.shape)
    packed = jnp.zeros((3, dp_count, section_count, slot_count, piece_rows, lane_count), jnp.float32)
    packed = packed.at[:, group_index, owners.astype(jnp.int32), position].set(states)
    packed = packed.reshape(3, dp_count, section_count * slot_count * piece_rows, lane_count)
    return (packed[0], packed[1], packed[2])
```

```python
import jax
import jax.numpy as jnp
from jax import lax
from jax.experimental import pallas as pl
from jax.experimental.pallas import tpu as pltpu
from jax.sharding import PartitionSpec as P

beta_one = 0.9
beta_two = 0.95
learn_rate = 0.03
decay_rate = 0.1
epsilon = 1e-08

LANE = 128
X, Z, CORE = 4, 12, 2
PAIR = 2
FAR = Z // PAIR
ROWS = 64
PIECES, PIECE = 8, 8
WRITERS, CAP = 8, 4
STATE = 3 * CAP * PIECE
BLOCK = STATE + PIECE


def device_of(x, z, core):
    return (x * Z + z) * CORE + core


def near_groups():
    return [
        [device_of(x, PAIR * a + b, c) for x in range(X) for b in range(PAIR)]
        for a in range(FAR)
        for c in range(CORE)
    ]


def far_groups():
    return [
        [device_of(x, PAIR * a + b, c) for a in range(FAR)]
        for x in range(X)
        for b in range(PAIR)
        for c in range(CORE)
    ]


def send_kernel(core_ref, grads_ref, out_ref):
    for a in range(FAR):
        for b in range(PAIR):
            first = grads_ref[0, 0, a, b, 0].astype(jnp.float32)
            out_ref[0, b, a] = first + grads_ref[1, 0, a, b, 0].astype(jnp.float32)


def join_kernel(core_ref, grads_ref, got_ref, out_ref):
    for a in range(FAR):
        for b in range(PAIR):
            first = grads_ref[0, 0, a, b, 0].astype(jnp.float32)
            own = first + grads_ref[1, 0, a, b, 0].astype(jnp.float32)
            out_ref[0, b, a] = own + got_ref[0, b, a]


def half_call(kernel, core, grads, *got):
    block = (1, PAIR, FAR, ROWS, LANE)
    stream = pl.BlockSpec(block, lambda i, core_ref: (i, 0, 0, 0, 0))
    return pl.pallas_call(
        kernel,
        out_shape=jax.ShapeDtypeStruct((X, PAIR, FAR, ROWS, LANE), jnp.float32),
        grid_spec=pltpu.PrefetchScalarGridSpec(
            num_scalar_prefetch=1,
            grid=(X,),
            in_specs=[
                pl.BlockSpec(
                    (2, 1, FAR, PAIR, 1, ROWS, LANE),
                    lambda i, core_ref: (0, i, 0, 0, core_ref[0], 0, 0),
                )
            ]
            + [stream] * len(got),
            out_specs=stream,
        ),
        cost_estimate=pl.CostEstimate(
            flops=2 * X * Z * ROWS * LANE,
            bytes_accessed=(8 + 4 * len(got)) * X * Z * ROWS * LANE,
            transcendentals=0,
        ),
    )(core, grads, *got)


def pack_kernel(owner_ref, parts_ref, params_ref, first_ref, second_ref, out_ref):
    gradient = parts_ref[0]
    for a in range(1, FAR):
        gradient = gradient + parts_ref[a]
    weights = params_ref[...]
    momentum = beta_one * first_ref[...] + (1.0 - beta_one) * gradient
    variance = beta_two * second_ref[...] + (1.0 - beta_two) * gradient * gradient
    updated = weights - learn_rate * (
        momentum / (jnp.sqrt(variance) + epsilon) + decay_rate * weights
    )
    owners = [owner_ref[p] for p in range(PIECES)]
    out_ref[...] = jnp.zeros_like(out_ref)
    for w in range(WRITERS):
        count = sum((owner == w).astype(jnp.int32) for owner in owners)
        out_ref[w, STATE:BLOCK] = jnp.full((PIECE, LANE), count.astype(jnp.float32))
    for p in range(PIECES):
        slot = jnp.int32(0)
        for q in range(p):
            slot = slot + (owners[q] == owners[p]).astype(jnp.int32)
        rows = slice(p * PIECE, (p + 1) * PIECE)
        for k, state in enumerate((updated, momentum, variance)):
            at = pl.multiple_of((slot + k * CAP) * PIECE, PIECE)
            out_ref[owners[p], pl.ds(at, PIECE)] = state[rows]


def place_kernel(got_ref, param_ref, first_ref, second_ref):
    outs = (param_ref, first_ref, second_ref)
    for out_ref in outs:
        out_ref[...] = jnp.zeros_like(out_ref)
    start = jnp.int32(0)
    for s in range(WRITERS):
        at = pl.multiple_of(start * PIECE, PIECE)
        for k, out_ref in enumerate(outs):
            rows = slice(k * CAP * PIECE, (k + 1) * CAP * PIECE)
            out_ref[0, pl.ds(at, CAP * PIECE)] = got_ref[s, rows]
        if s < WRITERS - 1:
            start = start + jnp.max(got_ref[s, STATE:BLOCK]).astype(jnp.int32)


def body(grads, params, first_moment, second_moment, owners):
    vmem = pl.BlockSpec(memory_space=pltpu.VMEM)
    smem = pl.BlockSpec(memory_space=pltpu.SMEM)
    core = lax.rem(lax.axis_index("dp"), CORE).astype(jnp.int32).reshape(1)
    grads = grads.reshape(2, X, FAR, PAIR, CORE, ROWS, LANE)
    sent = half_call(send_kernel, 1 - core, grads)
    swap = [(i, i ^ 1) for i in range(X * Z * CORE)]
    got = lax.ppermute(sent, "dp", swap)
    chip = half_call(join_kernel, core, grads, got)
    near = lax.all_to_all(
        chip.reshape(X * PAIR, FAR * ROWS, LANE), "dp", 0, 0, axis_index_groups=near_groups()
    )
    near = jnp.sum(near, axis=0).reshape(FAR, ROWS, LANE)
    far = lax.all_to_all(near, "dp", 0, 0, axis_index_groups=far_groups())
    packed = pl.pallas_call(
        pack_kernel,
        out_shape=jax.ShapeDtypeStruct((WRITERS, BLOCK, LANE), jnp.float32),
        in_specs=[smem] + [vmem] * 4,
        out_specs=vmem,
    )(owners.reshape(PIECES), far, params[0], first_moment[0], second_moment[0])
    handed = lax.all_to_all(packed, "section", 0, 0)
    out = jax.ShapeDtypeStruct((1, WRITERS * CAP * PIECE, LANE), jnp.float32)
    return pl.pallas_call(
        place_kernel,
        out_shape=(out,) * 3,
        in_specs=[vmem],
        out_specs=(vmem,) * 3,
    )(handed)


def solution(mesh):
    in_specs = (
        P("dp", None, "section", None, None),
        P("section", "dp", None),
        P("section", "dp", None),
        P("section", "dp", None),
        P("dp", "section", None),
    )
    out_specs = (P("dp", "section", None), P("dp", "section", None), P("dp", "section", None))
    return jax.shard_map(body, mesh=mesh, in_specs=in_specs, out_specs=out_specs, check_vma=False)
```

```python
import jax
import jax.numpy as jnp
from jax import lax
from jax.experimental import pallas as pl
from jax.experimental.pallas import tpu as pltpu
from jax.sharding import PartitionSpec as P

beta_one = 0.9
beta_two = 0.95
learn_rate = 0.03
decay_rate = 0.1
epsilon = 1e-08

LANE = 128
X, Z, CORE = 4, 12, 2
PAIR = 2
FAR = Z // PAIR
ROWS = 64
PIECES, PIECE = 8, 8
WRITERS, CAP = 8, 4
STATE = 3 * CAP * PIECE
BLOCK = STATE + PIECE


def device_of(x, z, core):
    return (x * Z + z) * CORE + core


def near_groups():
    return [
        [device_of(x, PAIR * a + b, c) for x in range(X) for b in range(PAIR)]
        for a in range(FAR)
        for c in range(CORE)
    ]


def far_groups():
    return [
        [device_of(x, PAIR * a + b, c) for a in range(FAR)]
        for x in range(X)
        for b in range(PAIR)
        for c in range(CORE)
    ]


def send_kernel(core_ref, grads_ref, out_ref):
    for a in range(FAR):
        for b in range(PAIR):
            first = grads_ref[0, 0, a, b, 0].astype(jnp.float32)
            out_ref[0, b, a] = first + grads_ref[1, 0, a, b, 0].astype(jnp.float32)


def join_kernel(core_ref, grads_ref, got_ref, out_ref):
    for a in range(FAR):
        for b in range(PAIR):
            first = grads_ref[0, 0, a, b, 0].astype(jnp.float32)
            own = first + grads_ref[1, 0, a, b, 0].astype(jnp.float32)
            out_ref[0, b, a] = own + got_ref[0, b, a]


def half_call(kernel, core, grads, *got):
    block = (1, PAIR, FAR, ROWS, LANE)
    stream = pl.BlockSpec(block, lambda i, core_ref: (i, 0, 0, 0, 0))
    return pl.pallas_call(
        kernel,
        out_shape=jax.ShapeDtypeStruct((X, PAIR, FAR, ROWS, LANE), jnp.float32),
        grid_spec=pltpu.PrefetchScalarGridSpec(
            num_scalar_prefetch=1,
            grid=(X,),
            in_specs=[
                pl.BlockSpec(
                    (2, 1, FAR, PAIR, 1, ROWS, LANE),
                    lambda i, core_ref: (0, i, 0, 0, core_ref[0], 0, 0),
                )
            ]
            + [stream] * len(got),
            out_specs=stream,
        ),
        compiler_params=pltpu.CompilerParams(vmem_limit_bytes=8 * 1024 * 1024),
        cost_estimate=pl.CostEstimate(
            flops=2 * X * Z * ROWS * LANE,
            bytes_accessed=(8 + 4 * len(got)) * X * Z * ROWS * LANE,
            transcendentals=0,
        ),
    )(core, grads, *got)


def pack_kernel(owner_ref, parts_ref, params_ref, first_ref, second_ref, out_ref):
    gradient = parts_ref[0]
    for a in range(1, FAR):
        gradient = gradient + parts_ref[a]
    weights = params_ref[...]
    momentum = beta_one * first_ref[...] + (1.0 - beta_one) * gradient
    variance = beta_two * second_ref[...] + (1.0 - beta_two) * gradient * gradient
    updated = weights - learn_rate * (
        momentum / (jnp.sqrt(variance) + epsilon) + decay_rate * weights
    )
    owners = [owner_ref[p] for p in range(PIECES)]
    out_ref[...] = jnp.zeros_like(out_ref)
    for w in range(WRITERS):
        count = sum((owner == w).astype(jnp.int32) for owner in owners)
        out_ref[w, STATE:BLOCK] = jnp.full((PIECE, LANE), count.astype(jnp.float32))
    for p in range(PIECES):
        slot = jnp.int32(0)
        for q in range(p):
            slot = slot + (owners[q] == owners[p]).astype(jnp.int32)
        rows = slice(p * PIECE, (p + 1) * PIECE)
        for k, state in enumerate((updated, momentum, variance)):
            at = pl.multiple_of((slot + k * CAP) * PIECE, PIECE)
            out_ref[owners[p], pl.ds(at, PIECE)] = state[rows]


def place_kernel(got_ref, param_ref, first_ref, second_ref):
    outs = (param_ref, first_ref, second_ref)
    for out_ref in outs:
        out_ref[...] = jnp.zeros_like(out_ref)
    start = jnp.int32(0)
    for s in range(WRITERS):
        at = pl.multiple_of(start * PIECE, PIECE)
        for k, out_ref in enumerate(outs):
            rows = slice(k * CAP * PIECE, (k + 1) * CAP * PIECE)
            out_ref[0, pl.ds(at, CAP * PIECE)] = got_ref[s, rows]
        if s < WRITERS - 1:
            start = start + jnp.max(got_ref[s, STATE:BLOCK]).astype(jnp.int32)


def body(grads, params, first_moment, second_moment, owners):
    vmem = pl.BlockSpec(memory_space=pltpu.VMEM)
    smem = pl.BlockSpec(memory_space=pltpu.SMEM)
    core = lax.rem(lax.axis_index("dp"), CORE).astype(jnp.int32).reshape(1)
    grads = grads.reshape(2, X, FAR, PAIR, CORE, ROWS, LANE)
    sent = half_call(send_kernel, 1 - core, grads)
    swap = [(i, i ^ 1) for i in range(X * Z * CORE)]
    got = lax.ppermute(sent, "dp", swap)
    chip = half_call(join_kernel, core, grads, got)
    near = lax.all_to_all(
        chip.reshape(X * PAIR, FAR * ROWS, LANE), "dp", 0, 0, axis_index_groups=near_groups()
    )
    near = jnp.sum(near, axis=0).reshape(FAR, ROWS, LANE)
    far = lax.all_to_all(near, "dp", 0, 0, axis_index_groups=far_groups())
    packed = pl.pallas_call(
        pack_kernel,
        out_shape=jax.ShapeDtypeStruct((WRITERS, BLOCK, LANE), jnp.float32),
        in_specs=[smem] + [vmem] * 4,
        out_specs=vmem,
        compiler_params=pltpu.CompilerParams(vmem_limit_bytes=8 * 1024 * 1024),
    )(owners.reshape(PIECES), far, params[0], first_moment[0], second_moment[0])
    handed = lax.all_to_all(packed, "section", 0, 0)
    out = jax.ShapeDtypeStruct((1, WRITERS * CAP * PIECE, LANE), jnp.float32)
    return pl.pallas_call(
        place_kernel,
        out_shape=(out,) * 3,
        in_specs=[vmem],
        out_specs=(vmem,) * 3,
        compiler_params=pltpu.CompilerParams(vmem_limit_bytes=8 * 1024 * 1024),
    )(handed)


def solution(mesh):
    in_specs = (
        P("dp", None, "section", None, None),
        P("section", "dp", None),
        P("section", "dp", None),
        P("section", "dp", None),
        P("dp", "section", None),
    )
    out_specs = (P("dp", "section", None), P("dp", "section", None), P("dp", "section", None))
    return jax.shard_map(body, mesh=mesh, in_specs=in_specs, out_specs=out_specs, check_vma=False)
```

```python
import jax
import jax.numpy as jnp
from jax import lax
from jax.experimental import pallas as pl
from jax.experimental.pallas import tpu as pltpu
from jax.sharding import PartitionSpec as P

beta_one = 0.9
beta_two = 0.95
learn_rate = 0.03
decay_rate = 0.1
epsilon = 1e-08

LANE = 128
X, Z, CORE = 4, 12, 2
PAIR = 2
FAR = Z // PAIR
ROWS = 64
PIECES, PIECE = 8, 8
WRITERS, CAP = 8, 4
HELD = CAP * PIECE
BLOCK = 3 * HELD
EMPTY = -1.0
LIMIT = 8 * 1024 * 1024


def device_of(x, z, core):
    return (x * Z + z) * CORE + core


def near_groups():
    return [
        [device_of(x, PAIR * a + b, c) for b in range(PAIR) for x in range(X)]
        for a in range(FAR)
        for c in range(CORE)
    ]


def far_groups():
    return [
        [device_of(x, PAIR * a + b, c) for a in range(FAR)]
        for x in range(X)
        for b in range(PAIR)
        for c in range(CORE)
    ]


def summed(grads_ref, x, a):
    first = grads_ref[0, x, a, 0, 0].astype(jnp.float32)
    return first + grads_ref[1, x, a, 0, 0].astype(jnp.float32)


def send_kernel(core_ref, grads_ref, out_ref):
    for x in range(X):
        for a in range(FAR):
            out_ref[0, x, a] = summed(grads_ref, x, a)


def join_kernel(core_ref, grads_ref, got_ref, out_ref):
    for x in range(X):
        for a in range(FAR):
            out_ref[0, x, a] = summed(grads_ref, x, a) + got_ref[0, x, a]


def half_call(kernel, core, grads, *got):
    stream = pl.BlockSpec((1, X, FAR, ROWS, LANE), lambda b, core_ref: (b, 0, 0, 0, 0))
    return pl.pallas_call(
        kernel,
        out_shape=jax.ShapeDtypeStruct((PAIR, X, FAR, ROWS, LANE), jnp.float32),
        grid_spec=pltpu.PrefetchScalarGridSpec(
            num_scalar_prefetch=1,
            grid=(PAIR,),
            in_specs=[
                pl.BlockSpec(
                    (2, X, FAR, 1, 1, ROWS, LANE),
                    lambda b, core_ref: (0, 0, 0, b, core_ref[0], 0, 0),
                )
            ]
            + [stream] * len(got),
            out_specs=stream,
        ),
        compiler_params=pltpu.CompilerParams(vmem_limit_bytes=LIMIT),
        cost_estimate=pl.CostEstimate(
            flops=2 * X * Z * ROWS * LANE,
            bytes_accessed=(8 + 4 * len(got)) * X * Z * ROWS * LANE,
            transcendentals=0,
        ),
    )(core, grads, *got)


def pack_kernel(owner_ref, parts_ref, params_ref, first_ref, second_ref, out_ref):
    gradient = parts_ref[0]
    for a in range(1, FAR):
        gradient = gradient + parts_ref[a]
    weights = params_ref[...]
    momentum = beta_one * first_ref[...] + (1.0 - beta_one) * gradient
    variance = beta_two * second_ref[...] + (1.0 - beta_two) * gradient * gradient
    updated = weights - learn_rate * (
        momentum / (jnp.sqrt(variance) + epsilon) + decay_rate * weights
    )
    owners = [owner_ref[p] for p in range(PIECES)]
    out_ref[:, : 2 * HELD] = jnp.zeros((WRITERS, 2 * HELD, LANE), jnp.float32)
    out_ref[:, 2 * HELD :] = jnp.full((WRITERS, HELD, LANE), EMPTY)
    for p in range(PIECES):
        slot = jnp.int32(0)
        for q in range(p):
            slot = slot + (owners[q] == owners[p]).astype(jnp.int32)
        rows = slice(p * PIECE, (p + 1) * PIECE)
        for k, state in enumerate((updated, momentum, variance)):
            at = pl.multiple_of((slot + k * CAP) * PIECE, PIECE)
            out_ref[owners[p], pl.ds(at, PIECE)] = state[rows]


def place_kernel(got_ref, param_ref, first_ref, second_ref):
    outs = (param_ref, first_ref, second_ref)
    for out_ref in outs:
        out_ref[...] = jnp.zeros_like(out_ref)
    start = jnp.int32(0)
    for s in range(WRITERS):
        at = pl.ds(pl.multiple_of(start * PIECE, PIECE), HELD)
        variance = got_ref[s, 2 * HELD :]
        param_ref[0, at] = got_ref[s, :HELD]
        first_ref[0, at] = got_ref[s, HELD : 2 * HELD]
        second_ref[0, at] = jnp.maximum(variance, 0.0)
        if s < WRITERS - 1:
            taken = sum(
                (variance[c * PIECE : (c + 1) * PIECE] >= 0.0).astype(jnp.int32)
                for c in range(CAP)
            )
            start = start + jnp.max(taken)


def body(grads, params, first_moment, second_moment, owners):
    vmem = pl.BlockSpec(memory_space=pltpu.VMEM)
    smem = pl.BlockSpec(memory_space=pltpu.SMEM)
    core = (lax.axis_index("dp").astype(jnp.int32) & 1).reshape(1)
    grads = grads.reshape(2, X, FAR, PAIR, CORE, ROWS, LANE)
    sent = half_call(send_kernel, core ^ 1, grads)
    swap = [(i, i ^ 1) for i in range(X * Z * CORE)]
    got = lax.ppermute(sent, "dp", swap)
    chip = half_call(join_kernel, core, grads, got)
    near = lax.all_to_all(
        chip.reshape(X * PAIR, FAR * ROWS, LANE), "dp", 0, 0, axis_index_groups=near_groups()
    )
    near = jnp.sum(near, axis=0).reshape(FAR, ROWS, LANE)
    far = lax.all_to_all(near, "dp", 0, 0, axis_index_groups=far_groups())
    packed = pl.pallas_call(
        pack_kernel,
        out_shape=jax.ShapeDtypeStruct((WRITERS, BLOCK, LANE), jnp.float32),
        in_specs=[smem] + [vmem] * 4,
        out_specs=vmem,
        compiler_params=pltpu.CompilerParams(vmem_limit_bytes=LIMIT),
    )(owners.reshape(PIECES), far, params[0], first_moment[0], second_moment[0])
    handed = lax.all_to_all(packed, "section", 0, 0)
    out = jax.ShapeDtypeStruct((1, WRITERS * CAP * PIECE, LANE), jnp.float32)
    return pl.pallas_call(
        place_kernel,
        out_shape=(out,) * 3,
        in_specs=[vmem],
        out_specs=(vmem,) * 3,
        compiler_params=pltpu.CompilerParams(vmem_limit_bytes=LIMIT),
    )(handed)


def solution(mesh):
    in_specs = (
        P("dp", None, "section", None, None),
        P("section", "dp", None),
        P("section", "dp", None),
        P("section", "dp", None),
        P("dp", "section", None),
    )
    out_specs = (P("dp", "section", None), P("dp", "section", None), P("dp", "section", None))
    return jax.shard_map(body, mesh=mesh, in_specs=in_specs, out_specs=out_specs, check_vma=False)
```

```python
import jax
import jax.numpy as jnp
from jax import lax
from jax.experimental import pallas as pl
from jax.experimental.pallas import tpu as pltpu
from jax.sharding import PartitionSpec as P

beta_one = 0.9
beta_two = 0.95
learn_rate = 0.03
decay_rate = 0.1
epsilon = 1e-08

LANE = 128
X, Z, CORE = 4, 12, 2
PAIR = 2
FAR = Z // PAIR
ROWS = 64
PIECES, PIECE = 8, 8
WRITERS, CAP = 8, 4
HELD = CAP * PIECE
BLOCK = 3 * HELD
EMPTY = -1.0
LIMIT = 8 * 1024 * 1024


def device_of(x, z, core):
    return (x * Z + z) * CORE + core


def z_of(a, side):
    return PAIR * a + (side ^ (a % 2))


def near_groups():
    return [
        [device_of(x, z_of(a, side), c) for side in range(PAIR) for x in range(X)]
        for a in range(FAR)
        for c in range(CORE)
    ]


def far_groups():
    return [
        [device_of(x, z_of(a, side), c) for a in range(FAR)]
        for x in range(X)
        for side in range(PAIR)
        for c in range(CORE)
    ]


def summed(grads_ref, x, k):
    first = grads_ref[0, x, k, 0, 0, 0].astype(jnp.float32)
    return first + grads_ref[1, x, k, 0, 0, 0].astype(jnp.float32)


def send_kernel(core_ref, even_ref, odd_ref, out_ref):
    for x in range(X):
        for k in range(FAR // 2):
            for parity, grads_ref in enumerate((even_ref, odd_ref)):
                out_ref[0, x, 2 * k + parity] = summed(grads_ref, x, k)


def join_kernel(core_ref, even_ref, odd_ref, got_ref, out_ref):
    for x in range(X):
        for k in range(FAR // 2):
            for parity, grads_ref in enumerate((even_ref, odd_ref)):
                a = 2 * k + parity
                out_ref[0, x, a] = summed(grads_ref, x, k) + got_ref[0, x, a]


def half_call(kernel, core, grads, *got):
    stream = pl.BlockSpec((1, X, FAR, ROWS, LANE), lambda side, core_ref: (side, 0, 0, 0, 0))
    block = (2, X, FAR // 2, 1, 1, 1, ROWS, LANE)
    even = pl.BlockSpec(block, lambda side, core_ref: (0, 0, 0, 0, side, core_ref[0], 0, 0))
    odd = pl.BlockSpec(block, lambda side, core_ref: (0, 0, 0, 1, 1 - side, core_ref[0], 0, 0))
    return pl.pallas_call(
        kernel,
        out_shape=jax.ShapeDtypeStruct((PAIR, X, FAR, ROWS, LANE), jnp.float32),
        grid_spec=pltpu.PrefetchScalarGridSpec(
            num_scalar_prefetch=1,
            grid=(PAIR,),
            in_specs=[even, odd] + [stream] * len(got),
            out_specs=stream,
        ),
        compiler_params=pltpu.CompilerParams(vmem_limit_bytes=LIMIT),
        cost_estimate=pl.CostEstimate(
            flops=2 * X * Z * ROWS * LANE,
            bytes_accessed=(8 + 4 * len(got)) * X * Z * ROWS * LANE,
            transcendentals=0,
        ),
    )(core, grads, grads, *got)


def pack_kernel(owner_ref, parts_ref, params_ref, first_ref, second_ref, out_ref):
    gradient = parts_ref[0]
    for a in range(1, FAR):
        gradient = gradient + parts_ref[a]
    weights = params_ref[...]
    momentum = beta_one * first_ref[...] + (1.0 - beta_one) * gradient
    variance = beta_two * second_ref[...] + (1.0 - beta_two) * gradient * gradient
    updated = weights - learn_rate * (
        momentum / (jnp.sqrt(variance) + epsilon) + decay_rate * weights
    )
    owners = [owner_ref[p] for p in range(PIECES)]
    out_ref[:, : 2 * HELD] = jnp.zeros((WRITERS, 2 * HELD, LANE), jnp.float32)
    out_ref[:, 2 * HELD :] = jnp.full((WRITERS, HELD, LANE), EMPTY)
    for p in range(PIECES):
        slot = jnp.int32(0)
        for q in range(p):
            slot = slot + (owners[q] == owners[p]).astype(jnp.int32)
        rows = slice(p * PIECE, (p + 1) * PIECE)
        for k, state in enumerate((updated, momentum, variance)):
            at = pl.multiple_of((slot + k * CAP) * PIECE, PIECE)
            out_ref[owners[p], pl.ds(at, PIECE)] = state[rows]


def place_kernel(got_ref, param_ref, first_ref, second_ref):
    outs = (param_ref, first_ref, second_ref)
    for out_ref in outs:
        out_ref[...] = jnp.zeros_like(out_ref)
    start = jnp.int32(0)
    for s in range(WRITERS):
        at = pl.ds(pl.multiple_of(start * PIECE, PIECE), HELD)
        variance = got_ref[s, 2 * HELD :]
        param_ref[0, at] = got_ref[s, :HELD]
        first_ref[0, at] = got_ref[s, HELD : 2 * HELD]
        second_ref[0, at] = jnp.maximum(variance, 0.0)
        if s < WRITERS - 1:
            taken = sum(
                (variance[c * PIECE : (c + 1) * PIECE] >= 0.0).astype(jnp.int32)
                for c in range(CAP)
            )
            start = start + jnp.max(taken)


def body(grads, params, first_moment, second_moment, owners):
    vmem = pl.BlockSpec(memory_space=pltpu.VMEM)
    smem = pl.BlockSpec(memory_space=pltpu.SMEM)
    core = (lax.axis_index("dp").astype(jnp.int32) & 1).reshape(1)
    grads = grads.reshape(2, X, FAR // 2, 2, PAIR, CORE, ROWS, LANE)
    sent = half_call(send_kernel, core ^ 1, grads)
    swap = [(i, i ^ 1) for i in range(X * Z * CORE)]
    got = lax.ppermute(sent, "dp", swap)
    chip = half_call(join_kernel, core, grads, got)
    near = lax.all_to_all(
        chip.reshape(X * PAIR, FAR * ROWS, LANE), "dp", 0, 0, axis_index_groups=near_groups()
    )
    near = jnp.sum(near, axis=0).reshape(FAR, ROWS, LANE)
    far = lax.all_to_all(near, "dp", 0, 0, axis_index_groups=far_groups())
    packed = pl.pallas_call(
        pack_kernel,
        out_shape=jax.ShapeDtypeStruct((WRITERS, BLOCK, LANE), jnp.float32),
        in_specs=[smem] + [vmem] * 4,
        out_specs=vmem,
        compiler_params=pltpu.CompilerParams(vmem_limit_bytes=LIMIT),
    )(owners.reshape(PIECES), far, params[0], first_moment[0], second_moment[0])
    handed = lax.all_to_all(packed, "section", 0, 0)
    out = jax.ShapeDtypeStruct((1, WRITERS * CAP * PIECE, LANE), jnp.float32)
    return pl.pallas_call(
        place_kernel,
        out_shape=(out,) * 3,
        in_specs=[vmem],
        out_specs=(vmem,) * 3,
        compiler_params=pltpu.CompilerParams(vmem_limit_bytes=LIMIT),
    )(handed)


def solution(mesh):
    in_specs = (
        P("dp", None, "section", None, None),
        P("section", "dp", None),
        P("section", "dp", None),
        P("section", "dp", None),
        P("dp", "section", None),
    )
    out_specs = (P("dp", "section", None), P("dp", "section", None), P("dp", "section", None))
    return jax.shard_map(body, mesh=mesh, in_specs=in_specs, out_specs=out_specs, check_vma=False)
```

```python
import jax
import jax.numpy as jnp
from jax import lax
from jax.experimental import pallas as pl
from jax.experimental.pallas import tpu as pltpu
from jax.sharding import PartitionSpec as P

beta_one = 0.9
beta_two = 0.95
learn_rate = 0.03
decay_rate = 0.1
epsilon = 1e-08

LANE = 128
X, Z, CORE = 4, 12, 2
PAIR = 2
FAR = Z // PAIR
ROWS = 64
PIECES, PIECE = 8, 8
WRITERS, CAP = 8, 4
HELD = CAP * PIECE
BLOCK = 3 * HELD
EMPTY = -1.0
LIMIT = 8 * 1024 * 1024


def device_of(x, z, core):
    return (x * Z + z) * CORE + core


def z_of(a, side):
    return PAIR * a + (side ^ (a % 2))


def near_groups():
    return [
        [device_of(x, z_of(a, side), c) for side in range(PAIR) for x in range(X)]
        for a in range(FAR)
        for c in range(CORE)
    ]


def far_groups():
    return [
        [device_of(x, z_of(a, side), c) for a in range(FAR)]
        for x in range(X)
        for side in range(PAIR)
        for c in range(CORE)
    ]


def summed(grads_ref, core, side, x, a):
    at = (x, a // 2, a % 2, side ^ (a % 2), core)
    return grads_ref[(0, *at)].astype(jnp.float32) + grads_ref[(1, *at)].astype(jnp.float32)


def send_kernel(core_ref, grads_ref, out_ref):
    for side in range(PAIR):
        for x in range(X):
            for a in range(FAR):
                out_ref[side, x, a] = summed(grads_ref, core_ref[0], side, x, a)


def join_kernel(core_ref, grads_ref, got_ref, out_ref):
    for side in range(PAIR):
        for x in range(X):
            for a in range(FAR):
                own = summed(grads_ref, core_ref[0], side, x, a)
                out_ref[side, x, a] = own + got_ref[side, x, a]


def half_call(kernel, core, grads, *got):
    vmem = pl.BlockSpec(memory_space=pltpu.VMEM)
    return pl.pallas_call(
        kernel,
        out_shape=jax.ShapeDtypeStruct((PAIR, X, FAR, ROWS, LANE), jnp.float32),
        in_specs=[pl.BlockSpec(memory_space=pltpu.SMEM), vmem] + [vmem] * len(got),
        out_specs=vmem,
        compiler_params=pltpu.CompilerParams(vmem_limit_bytes=2 * LIMIT),
        cost_estimate=pl.CostEstimate(
            flops=2 * X * Z * ROWS * LANE,
            bytes_accessed=(8 + 4 * len(got)) * X * Z * ROWS * LANE,
            transcendentals=0,
        ),
    )(core, grads, *got)


def pack_kernel(owner_ref, parts_ref, params_ref, first_ref, second_ref, out_ref):
    gradient = parts_ref[0]
    for a in range(1, FAR):
        gradient = gradient + parts_ref[a]
    weights = params_ref[...]
    momentum = beta_one * first_ref[...] + (1.0 - beta_one) * gradient
    variance = beta_two * second_ref[...] + (1.0 - beta_two) * gradient * gradient
    updated = weights - learn_rate * (
        momentum / (jnp.sqrt(variance) + epsilon) + decay_rate * weights
    )
    owners = [owner_ref[p] for p in range(PIECES)]
    out_ref[:, : 2 * HELD] = jnp.zeros((WRITERS, 2 * HELD, LANE), jnp.float32)
    out_ref[:, 2 * HELD :] = jnp.full((WRITERS, HELD, LANE), EMPTY)
    for p in range(PIECES):
        slot = jnp.int32(0)
        for q in range(p):
            slot = slot + (owners[q] == owners[p]).astype(jnp.int32)
        rows = slice(p * PIECE, (p + 1) * PIECE)
        for k, state in enumerate((updated, momentum, variance)):
            at = pl.multiple_of((slot + k * CAP) * PIECE, PIECE)
            out_ref[owners[p], pl.ds(at, PIECE)] = state[rows]


def place_kernel(got_ref, param_ref, first_ref, second_ref):
    outs = (param_ref, first_ref, second_ref)
    for out_ref in outs:
        out_ref[...] = jnp.zeros_like(out_ref)
    start = jnp.int32(0)
    for s in range(WRITERS):
        at = pl.ds(pl.multiple_of(start * PIECE, PIECE), HELD)
        variance = got_ref[s, 2 * HELD :]
        param_ref[0, at] = got_ref[s, :HELD]
        first_ref[0, at] = got_ref[s, HELD : 2 * HELD]
        second_ref[0, at] = jnp.maximum(variance, 0.0)
        if s < WRITERS - 1:
            taken = sum(
                (variance[c * PIECE : (c + 1) * PIECE] >= 0.0).astype(jnp.int32)
                for c in range(CAP)
            )
            start = start + jnp.max(taken)


def body(grads, params, first_moment, second_moment, owners):
    vmem = pl.BlockSpec(memory_space=pltpu.VMEM)
    smem = pl.BlockSpec(memory_space=pltpu.SMEM)
    core = (lax.axis_index("dp").astype(jnp.int32) & 1).reshape(1)
    grads = grads.reshape(2, X, FAR // 2, 2, PAIR, CORE, ROWS, LANE)
    sent = half_call(send_kernel, core ^ 1, grads)
    swap = [(i, i ^ 1) for i in range(X * Z * CORE)]
    got = lax.ppermute(sent, "dp", swap)
    chip = half_call(join_kernel, core, grads, got)
    near = lax.all_to_all(
        chip.reshape(X * PAIR, FAR * ROWS, LANE), "dp", 0, 0, axis_index_groups=near_groups()
    )
    near = jnp.sum(near, axis=0).reshape(FAR, ROWS, LANE)
    far = lax.all_to_all(near, "dp", 0, 0, axis_index_groups=far_groups())
    packed = pl.pallas_call(
        pack_kernel,
        out_shape=jax.ShapeDtypeStruct((WRITERS, BLOCK, LANE), jnp.float32),
        in_specs=[smem] + [vmem] * 4,
        out_specs=vmem,
        compiler_params=pltpu.CompilerParams(vmem_limit_bytes=LIMIT),
    )(owners.reshape(PIECES), far, params[0], first_moment[0], second_moment[0])
    handed = lax.all_to_all(packed, "section", 0, 0)
    out = jax.ShapeDtypeStruct((1, WRITERS * CAP * PIECE, LANE), jnp.float32)
    return pl.pallas_call(
        place_kernel,
        out_shape=(out,) * 3,
        in_specs=[vmem],
        out_specs=(vmem,) * 3,
        compiler_params=pltpu.CompilerParams(vmem_limit_bytes=LIMIT),
    )(handed)


def solution(mesh):
    in_specs = (
        P("dp", None, "section", None, None),
        P("section", "dp", None),
        P("section", "dp", None),
        P("section", "dp", None),
        P("dp", "section", None),
    )
    out_specs = (P("dp", "section", None), P("dp", "section", None), P("dp", "section", None))
    return jax.shard_map(body, mesh=mesh, in_specs=in_specs, out_specs=out_specs, check_vma=False)
```
